32 devices in a mesh: rep: 2 (over y), grp: 4 (over z), loc: 4 (over x, core).
Axes of the slice: x: 2, y: 2, z: 4, core: 2. Of those that a mesh axis runs over, the one named last changes fastest.
Arguments:
- tokens: bfloat16 [4096, 3584], P(('rep', 'grp', 'loc')), parts along dimension 0, may hold values from -6 to 6
- expert_ids: int32 [4096, 8], P(('rep', 'grp', 'loc')), parts along dimension 0, may hold values from 0 to 255, as said below
- route_weights: float32 [4096, 8], P(('rep', 'grp', 'loc')), parts along dimension 0, may hold values from 0.5 to 2.5
- w_gate: bfloat16 [3584, 32768], P(None, ('grp', 'loc')), may hold values from -0.09375 to 0.09375
- w_up: bfloat16 [3584, 32768], P(None, ('grp', 'loc')), may hold values from -0.09375 to 0.09375
- w_down: bfloat16 [3584, 32768], P(None, ('grp', 'loc')), may hold values from -0.1875 to 0.1875
Outputs:
- routed_out: bfloat16 [4096, 3584], P(('rep', 'grp', 'loc')), parts along dimension 0
The draws below stay inside these ranges and needn't reach their ends.
There are 2 independent parts, one for each index of `rep`. The reference program is written for one: setup_inputs(seed, part) draws one part's arguments, and reference() takes and returns one part's arrays. A program takes and returns all parts, laid end to end along the dimension named above; an argument that names none is the same for every part. Nothing has to cross between parts.
Inputs may be any that keep to these rules, and one draw needn't show every extreme that they name: `expert_ids`: each row names 8 different experts, lying in at most 4 of the 8 groups of 32 consecutive ids, and at most one id below 32. In each aligned block of 128 rows (the rows of one device) every id below 32 is named by at most 4 rows, and one such id, the same in every block, by exactly 4.
All inputs are finite; a program needn't handle non-finite values.
Results may differ from the reference program's by a relative error of at most 0.005.
Values may be sent and summed in bfloat16 or wider, within the bound.
A program may use at most 320 MiB of HBM per device.

```python
import jax
import jax.numpy as jnp
from jax import lax

D = 3584
FF = 1024
EXPERTS = 256
GROUPS = 8
TOPG = 4
TOP = 8
TOK_DEV = 128
EXP_WIN = 32
TOKENS = 2048
CAP = 4


def permute_tokens(sub_key):
    return jax.random.permutation(sub_key, TOK_DEV)


def shuffle_groups(sub_key):
    return jax.random.permutation(sub_key, GROUPS - 1)[:TOPG - 1] + 1


def pick_positions(sub_key):
    return jax.random.permutation(sub_key, (TOPG - 1) * (EXPERTS // GROUPS))[:TOP]


def draw_expert_ids(key, part):
    key = jax.random.fold_in(key, 11)
    blocks = TOKENS // TOK_DEV
    group_size = EXPERTS // GROUPS
    subkeys = jax.random.split(key, 6)
    hot_expert = jax.random.randint(subkeys[0], (), 0, EXP_WIN)
    counts = jax.random.randint(subkeys[1], (blocks, EXP_WIN), 0, CAP + 1)
    counts = jnp.where(jnp.arange(EXP_WIN)[None, :] == hot_expert, CAP, counts)
    position = jnp.arange(TOK_DEV)
    pos_exp = jnp.minimum(position // CAP, EXP_WIN - 1)
    in_range = position < EXP_WIN * CAP
    pos_cnt = counts[:, pos_exp]
    live_slot = in_range[None, :] & ((position % CAP)[None, :] < pos_cnt)
    window = jnp.where(live_slot, pos_exp[None, :], -1)
    orders = jax.vmap(permute_tokens)(jax.random.split(subkeys[2], blocks))
    window = jnp.take_along_axis(window, orders, 1).reshape(-1)
    others = jax.vmap(shuffle_groups)(jax.random.split(subkeys[3], TOKENS))
    drawn_pos = jax.vmap(pick_positions)(jax.random.split(subkeys[4], TOKENS))
    group_of = jnp.take_along_axis(others, drawn_pos // group_size, 1)
    experts = group_of * group_size + drawn_pos % group_size
    column = jax.random.randint(subkeys[5], (TOKENS,), 0, TOP)
    replace = (window >= 0)[:, None] & (jnp.arange(TOP)[None, :] == column[:, None])
    expert_ids = jnp.where(replace, window[:, None], experts)
    return expert_ids.astype(jnp.int32)


def shard_levels(own_key, extent, shards, smallest, top_value):
    level, own = 1.0, jax.random.fold_in(own_key, 6)
    for axis_at, shards_of in shards:
        steps = jnp.exp(jax.random.uniform(jax.random.fold_in(own, axis_at), (shards_of,), jnp.float32, smallest / len(shards), top_value / len(shards)))
        level = level * jnp.repeat(steps, extent[axis_at] // shards_of).reshape([-1 if axis == axis_at else 1 for axis in range(len(extent))])
    return level


def noise(key, dims, scale, bound, cuts=(), held_as=jnp.bfloat16):
    entries = scale * jax.random.normal(key, dims, jnp.float32)
    if cuts:
        entries = entries * shard_levels(key, dims, cuts, -0.22, 0.18)
    return jnp.clip(entries, -bound, bound).astype(held_as)


def setup_inputs(seed: int = 0, part: int = 0) -> dict:
    key_of = jax.random.split(jax.random.key(seed), 7)
    part_splits = jax.random.split(jax.random.fold_in(key_of[6], part), 7)
    return {
        "tokens": noise(part_splits[0], (TOKENS, D), 1.0, 6.0, ((0, 16),)),
        "expert_ids": draw_expert_ids(jax.random.fold_in(jax.random.fold_in(key_of[6], part), 71), part),
        "route_weights": jnp.clip(0.5 + 2.0 * jax.random.uniform(part_splits[2], (TOKENS, TOP), jnp.float32) ** shard_levels(part_splits[2], (TOKENS, TOP), ((0, 16),), -0.2, 0.2), 0.5, 2.5),
        "w_gate": noise(key_of[3], (D, EXP_WIN * FF), D ** -0.5, 0.09375, ((1, 16),)),
        "w_up": noise(key_of[4], (D, EXP_WIN * FF), D ** -0.5, 0.09375, ((1, 16),)),
        "w_down": noise(key_of[5], (D, EXP_WIN * FF), FF ** -0.5, 0.1875, ((1, 16),)),
    }


def reference(tokens, expert_ids, route_weights, w_gate, w_up, w_down):
    most_rows = (TOKENS // TOK_DEV) * CAP
    padded = jnp.concatenate([tokens, jnp.zeros((1, D), tokens.dtype)], 0)
    chosen = jnp.where(expert_ids < EXP_WIN, expert_ids, -1)

    def one_expert(expert_idx, running):
        expert_idx = jnp.asarray(expert_idx).astype(jnp.int32)
        matched = chosen == expert_idx
        coefficient = jnp.sum(jnp.where(matched, route_weights, 0.0), 1)
        coefficient_pad = jnp.concatenate([coefficient, jnp.zeros((1,), coefficient.dtype)])
        row_index = jnp.nonzero(jnp.any(matched, 1), size=most_rows, fill_value=TOKENS)[0].astype(jnp.int32)
        picked = padded[row_index]
        col_start = (expert_idx * FF).astype(jnp.int32)
        gate_cols = lax.dynamic_slice_in_dim(w_gate, col_start, FF, 1)
        up_cols = lax.dynamic_slice_in_dim(w_up, col_start, FF, 1)
        down_cols = lax.dynamic_slice_in_dim(w_down, col_start, FF, 1)
        gate_act = jnp.dot(picked, gate_cols, preferred_element_type=jnp.float32)
        up_act = jnp.dot(picked, up_cols, preferred_element_type=jnp.float32)
        hidden = (jax.nn.silu(gate_act) * up_act).astype(jnp.bfloat16)
        expert_out = jnp.dot(hidden, down_cols.T, preferred_element_type=jnp.float32)
        return running.at[row_index].add(expert_out * coefficient_pad[row_index][:, None])

    running = lax.fori_loop(0, EXP_WIN, one_expert, jnp.zeros((TOKENS + 1, D), jnp.float32))
    return running[:TOKENS].astype(jnp.bfloat16)
```

```python
import functools

import jax
import jax.numpy as jnp
from jax import lax
from jax.experimental import pallas as pl
from jax.experimental.pallas import tpu as pltpu
from jax.sharding import PartitionSpec as P

FF = 1024
EXP_WIN = 32
TILE = 16
MESH = pl.DeviceIdType.MESH


def iota(shape, dim):
    return lax.broadcasted_iota(jnp.int32, shape, dim)


def experts_kernel(
    groups, loc_ranks, own_exp, cap, quarters,
    ids_ref, weight_ref, tokens_ref, gate_ref, up_ref, down_ref, out_ref,
    tok, wg, wu, wd, place, send, recv, rows, hidden, stacked, ysend, yrecv, part,
    tok_sem, w_sem, self_sem, send_sem, recv_sem, yself_sem, ysend_sem, yrecv_sem,
):
    devices = groups * loc_ranks
    tok_dev = tok.shape[0] // quarters
    quarter = tok.shape[1]
    slots = devices * cap
    z, l = lax.axis_index("grp"), lax.axis_index("loc")
    me = z * loc_ranks + l

    def token_copy(q):
        return pltpu.make_async_copy(
            tokens_ref.at[:, pl.ds(q * quarter, quarter)],
            tok.at[pl.ds(q * tok_dev, tok_dev)],
            tok_sem.at[q],
        )

    def weight_copy(m, j):
        from_ref, to_ref = ((gate_ref, wg), (up_ref, wu), (down_ref, wd))[m]
        return pltpu.make_async_copy(
            from_ref.at[:, pl.ds(j * FF, FF)], to_ref.at[j], w_sem.at[m, j]
        )

    for q in range(quarters):
        token_copy(q).start()
    for j in range(own_exp):
        for m in range(3):
            weight_copy(m, j).start()

    def each_peer(act):
        mirror = groups - 1 - z
        for zz, first in (
            [(mirror, 0)]
            + [(lax.rem(mirror + d, groups), 0) for d in range(1, groups)]
        ):
            def step(d, carry, zz=zz):
                ll = lax.rem(l + d, loc_ranks)

                @pl.when(zz * loc_ranks + ll != me)
                def _():
                    act(zz, ll, zz * loc_ranks + ll)

                return carry

            lax.fori_loop(first, loc_ranks, step, 0)

    barrier = pltpu.get_barrier_semaphore()

    def greet(zz, ll, peer):
        pl.semaphore_signal(
            barrier, inc=1, device_id={"grp": zz, "loc": ll}, device_id_type=MESH
        )

    each_peer(greet)

    ids = ids_ref[...]
    inside = ids < EXP_WIN
    expert = jnp.min(jnp.where(inside, ids, EXP_WIN), 0, keepdims=True)
    onehot = (iota((EXP_WIN, tok_dev), 0) == expert).astype(jnp.float32)
    earlier = (iota((tok_dev, tok_dev), 0) < iota((tok_dev, tok_dev), 1)).astype(jnp.bfloat16)
    before = jnp.dot(onehot.astype(jnp.bfloat16), earlier, preferred_element_type=jnp.float32)
    rank = jnp.sum(before * onehot, 0, keepdims=True).astype(jnp.int32)
    weight_row = jnp.sum(jnp.where(inside, weight_ref[...], 0.0), 0, keepdims=True)
    diagonal = iota((tok_dev, tok_dev), 0) == iota((tok_dev, tok_dev), 1)
    weight = jnp.sum(jnp.where(diagonal, weight_row, 0.0), 1, keepdims=True)
    for j in range(own_exp):
        for q in range(quarters):
            target = jnp.full_like(expert, -1)
            for d in range(devices):
                target = jnp.where(expert == d * own_exp + j, d * TILE + q * cap + rank, target)
            place[j, :, pl.ds(q * tok_dev, tok_dev)] = (
                iota((devices * TILE, tok_dev), 0) == target
            ).astype(jnp.bfloat16)
    row, col = iota((devices * TILE, devices * TILE), 0), iota((devices * TILE, devices * TILE), 1)
    home = jnp.zeros_like(row)
    for q in range(quarters):
        for d in range(devices):
            start = q * slots + d * cap
            home = jnp.where((row >= start) & (row < start + cap), row - start + d * TILE + q * cap, home)
    spread_out = (col == home).astype(jnp.bfloat16)
    home = jnp.zeros_like(row)
    for q in range(quarters):
        for d in range(devices):
            start = q * slots + d * cap
            home = jnp.where((col >= start) & (col < start + cap), col - start + d * TILE + q * cap, home)
    gather_in = (row == home).astype(jnp.bfloat16)

    for q in range(quarters):
        token_copy(q).wait()

    def forward(j, zz, ll, peer):
        return pltpu.make_async_remote_copy(
            src_ref=send.at[j, peer], dst_ref=recv.at[j, me],
            send_sem=send_sem.at[j, peer], recv_sem=recv_sem.at[j, me],
            device_id={"grp": zz, "loc": ll}, device_id_type=MESH,
        )

    def arrived(j, zz, ll, peer):
        return pltpu.make_async_remote_copy(
            src_ref=send.at[j, peer], dst_ref=recv.at[j, peer],
            send_sem=send_sem.at[j, peer], recv_sem=recv_sem.at[j, peer],
            device_id={"grp": zz, "loc": ll}, device_id_type=MESH,
        )

    def back(j, zz, ll, peer):
        return pltpu.make_async_remote_copy(
            src_ref=ysend.at[j, peer], dst_ref=yrecv.at[j, me],
            send_sem=ysend_sem.at[j, peer], recv_sem=yrecv_sem.at[j, me],
            device_id={"grp": zz, "loc": ll}, device_id_type=MESH,
        )

    def returned(j, zz, ll, peer):
        return pltpu.make_async_remote_copy(
            src_ref=ysend.at[j, peer], dst_ref=yrecv.at[j, peer],
            send_sem=ysend_sem.at[j, peer], recv_sem=yrecv_sem.at[j, peer],
            device_id={"grp": zz, "loc": ll}, device_id_type=MESH,
        )

    def own_forward(j):
        return pltpu.make_async_copy(send.at[j, me], recv.at[j, me], self_sem.at[j])

    def own_back(j):
        return pltpu.make_async_copy(ysend.at[j, me], yrecv.at[j, me], yself_sem.at[j])

    for j in range(own_exp):
        picked = jnp.dot(place[j], tok[...], preferred_element_type=jnp.float32)
        send[j] = picked.astype(jnp.bfloat16).reshape(devices, TILE, quarter)
        if j == 0:
            pl.semaphore_wait(barrier, devices - 1)
        each_peer(lambda zz, ll, peer: forward(j, zz, ll, peer).start())
        own_forward(j).start()

    step = 256
    for j in range(own_exp):
        each_peer(lambda zz, ll, peer: arrived(j, zz, ll, peer).wait_recv())
        own_forward(j).wait()
        ordered = jnp.dot(
            spread_out, recv[j].reshape(devices * TILE, quarter),
            preferred_element_type=jnp.float32,
        ).astype(jnp.bfloat16)
        for q in range(quarters):
            rows[:, pl.ds(q * quarter, quarter)] = ordered[q * slots : (q + 1) * slots]
        weight_copy(0, j).wait()
        weight_copy(1, j).wait()

        def gate_up(n, carry):
            at = pl.ds(pl.multiple_of(n * step, step), step)
            gate = jnp.dot(rows[...], wg[j, :, at], preferred_element_type=jnp.float32)
            up = jnp.dot(rows[...], wu[j, :, at], preferred_element_type=jnp.float32)
            hidden[:, at] = (gate / (1.0 + jnp.exp(-gate)) * up).astype(jnp.bfloat16)
            return carry

        lax.fori_loop(0, FF // step, gate_up, 0)
        weight_copy(2, j).wait()

        def down(q, carry):
            product = lax.dot_general(
                hidden[...], wd[j, pl.ds(pl.multiple_of(q * quarter, quarter), quarter), :],
                (((1,), (1,)), ((), ())), preferred_element_type=jnp.float32,
            )
            stacked[pl.ds(pl.multiple_of(q * slots, slots), slots), :] = product.astype(jnp.bfloat16)
            return carry

        lax.fori_loop(0, quarters, down, 0)
        ysend[j] = (
            jnp.dot(gather_in, stacked[...], preferred_element_type=jnp.float32)
            .astype(jnp.bfloat16)
            .reshape(devices, TILE, quarter)
        )
        each_peer(lambda zz, ll, peer: back(j, zz, ll, peer).start())
        own_back(j).start()

    for j in range(own_exp):
        each_peer(lambda zz, ll, peer: returned(j, zz, ll, peer).wait_recv())
        own_back(j).wait()
        blocks = yrecv[j].reshape(devices * TILE, quarter)
        for q in range(quarters):
            at = pl.ds(q * quarter, quarter)
            chosen = lax.dot_general(
                place[j, :, pl.ds(q * tok_dev, tok_dev)], blocks,
                (((0,), (0,)), ((), ())), preferred_element_type=jnp.float32,
            )
            if j > 0:
                chosen = chosen + part[:, at].astype(jnp.float32)
            if j < own_exp - 1:
                part[:, at] = chosen.astype(jnp.bfloat16)
            else:
                out_ref[:, at] = (chosen * weight).astype(jnp.bfloat16)

    for j in range(own_exp):
        each_peer(lambda zz, ll, peer: forward(j, zz, ll, peer).wait_send())
        each_peer(lambda zz, ll, peer: back(j, zz, ll, peer).wait_send())


def whole_experts(tokens, expert_ids, route_weights, w_gate, w_up, w_down):
    tok_dev, width = tokens.shape
    cap = tok_dev // EXP_WIN
    groups, loc_ranks = lax.axis_size("grp"), lax.axis_size("loc")
    devices = groups * loc_ranks
    own_exp = w_gate.shape[1] // FF
    quarters = TILE // cap
    quarter = width // quarters
    slots = devices * cap
    bf16 = jnp.bfloat16
    anywhere, vmem = pl.BlockSpec(memory_space=pl.ANY), pl.BlockSpec(memory_space=pltpu.VMEM)
    dma = pltpu.SemaphoreType.DMA
    block = pltpu.VMEM((own_exp, devices, TILE, quarter), bf16)
    return pl.pallas_call(
        functools.partial(experts_kernel, groups, loc_ranks, own_exp, cap, quarters),
        out_shape=jax.ShapeDtypeStruct((tok_dev, width), bf16),
        in_specs=[vmem, vmem, anywhere, anywhere, anywhere, anywhere],
        out_specs=vmem,
        scratch_shapes=[
            pltpu.VMEM((quarters * tok_dev, quarter), bf16),
            pltpu.VMEM((own_exp, width, FF), bf16),
            pltpu.VMEM((own_exp, width, FF), bf16),
            pltpu.VMEM((own_exp, width, FF), bf16),
            pltpu.VMEM((own_exp, devices * TILE, quarters * tok_dev), bf16),
            block,
            block,
            pltpu.VMEM((slots, width), bf16),
            pltpu.VMEM((slots, FF), bf16),
            pltpu.VMEM((quarters * slots, quarter), bf16),
            block,
            block,
            pltpu.VMEM((tok_dev, width), bf16),
            dma((quarters,)),
            dma((3, own_exp)),
            dma((own_exp,)),
            dma((own_exp, devices)),
            dma((own_exp, devices)),
            dma((own_exp,)),
            dma((own_exp, devices)),
            dma((own_exp, devices)),
        ],
        compiler_params=pltpu.CompilerParams(
            collective_id=0, has_side_effects=True, vmem_limit_bytes=60 * 2**20
        ),
        cost_estimate=pl.CostEstimate(
            flops=6 * slots * own_exp * width * FF,
            bytes_accessed=6 * own_exp * width * FF,
            transcendentals=slots * own_exp * FF,
        ),
    )(expert_ids.T, route_weights.T, tokens, w_gate, w_up, w_down)


def send_back(partial_value):
    return lax.all_to_all(partial_value, "grp", split_axis=0, concat_axis=0, tiled=True)


def split_experts(tokens, expert_ids, route_weights, w_gate, w_up, w_down):
    tok_dev, model_width = tokens.shape
    capacity = tok_dev // EXP_WIN
    groups = lax.axis_size("grp")
    loc_ranks = lax.axis_size("loc")
    hid_dev = w_gate.shape[1]
    hid_grp = hid_dev * loc_ranks
    hid_exp = min(FF, hid_grp)
    per_grp = hid_grp // hid_exp
    spread = FF // hid_exp
    slot_count = EXP_WIN * spread * capacity
    flat_ids = expert_ids.reshape(-1)
    flat_weight = route_weights.reshape(-1)
    owner_tok = jnp.arange(flat_ids.shape[0], dtype=jnp.int32) // expert_ids.shape[1]
    inside = flat_ids < EXP_WIN
    onehot = (
        (flat_ids[:, None] == jnp.arange(EXP_WIN, dtype=jnp.int32)[None, :]) & inside[:, None]
    ).astype(jnp.int32)
    before = jnp.cumsum(onehot, 0) - onehot
    rank_in = jnp.sum(before * onehot, 1)
    slot_tok = jnp.full((slot_count + 1,), tok_dev, jnp.int32)
    slot_weight = jnp.zeros((slot_count + 1,), jnp.float32)
    for copy_idx in range(spread):
        where_to = jnp.where(
            inside, (flat_ids * spread + copy_idx) * capacity + rank_in, slot_count
        )
        slot_tok = slot_tok.at[where_to].set(owner_tok)
        slot_weight = slot_weight.at[where_to].set(flat_weight)
    slot_tok = slot_tok[:slot_count]
    slot_weight = slot_weight[:slot_count]
    padded = jnp.concatenate([tokens, jnp.zeros((1, model_width), tokens.dtype)], 0)
    outgoing = padded[slot_tok].reshape(groups, per_grp, capacity, model_width)
    full_down = lax.all_gather(w_down, "loc", axis=1, tiled=True)
    down_cols = full_down.reshape(model_width, per_grp, hid_exp)
    own_exp = max(1, hid_dev // hid_exp)
    own_width = min(hid_dev, hid_exp)
    first_exp = lax.axis_index("loc") * hid_dev // hid_exp
    gate_cols = w_gate.reshape(model_width, own_exp, own_width)
    up_cols = w_up.reshape(model_width, own_exp, own_width)
    everyone = lax.all_gather(
        lax.all_to_all(outgoing, "grp", split_axis=0, concat_axis=0, tiled=True),
        "loc",
        axis=0,
        tiled=True,
    )
    own_rows = lax.dynamic_slice_in_dim(everyone, first_exp, own_exp, 1)
    gate_act = jnp.einsum("njkd,dji->nkji", own_rows, gate_cols, preferred_element_type=jnp.float32)
    up_act = jnp.einsum("njkd,dji->nkji", own_rows, up_cols, preferred_element_type=jnp.float32)
    hidden = (jax.nn.silu(gate_act) * up_act).astype(jnp.bfloat16)
    hidden = hidden.reshape(hidden.shape[0], hidden.shape[1], own_exp * own_width)
    shared = lax.all_to_all(hidden, "loc", split_axis=0, concat_axis=2, tiled=True)
    shared = shared.reshape(shared.shape[0], shared.shape[1], per_grp, hid_exp)
    partial_value = jnp.einsum(
        "skje,dje->sjkd", shared, down_cols, preferred_element_type=jnp.float32
    )
    returned = send_back(partial_value)
    returned = returned.reshape(slot_count, model_width)
    combined = (
        jnp.zeros((tok_dev + 1, model_width), jnp.float32)
        .at[slot_tok]
        .add(returned * slot_weight[:, None])
    )
    return combined[:tok_dev].astype(jnp.bfloat16)


def local(tokens, expert_ids, route_weights, w_gate, w_up, w_down):
    tok_dev, width = tokens.shape
    devices = lax.axis_size("grp") * lax.axis_size("loc")
    cap = tok_dev // EXP_WIN
    whole = (
        w_gate.shape[1] % FF == 0
        and devices * w_gate.shape[1] == EXP_WIN * FF
        and tok_dev % EXP_WIN == 0
        and tok_dev % 128 == 0
        and TILE % cap == 0
        and width % (128 * (TILE // cap)) == 0
    )
    plan = whole_experts if whole else split_experts
    return plan(tokens, expert_ids, route_weights, w_gate, w_up, w_down)


def solution(mesh):
    placed = (
        P(("rep", "grp", "loc"), None),
        P(("rep", "grp", "loc"), None),
        P(("rep", "grp", "loc"), None),
        P(None, ("grp", "loc")),
        P(None, ("grp", "loc")),
        P(None, ("grp", "loc")),
    )
    return jax.shard_map(
        local, mesh=mesh, in_specs=placed, out_specs=P(("rep", "grp", "loc"), None), check_vma=False
    )
```

```python
import functools

import jax
import jax.numpy as jnp
from jax import lax
from jax.experimental import pallas as pl
from jax.experimental.pallas import tpu as pltpu
from jax.sharding import PartitionSpec as P

FF = 1024
EXP_WIN = 32
TILE = 16
MESH = pl.DeviceIdType.MESH


def iota(shape, dim):
    return lax.broadcasted_iota(jnp.int32, shape, dim)


def quotient(values, power_of_two):
    return lax.shift_right_logical(values, power_of_two.bit_length() - 1)


def experts_kernel(
    groups, loc_ranks, own_exp, cap, quarters,
    ids_ref, weight_ref, tokens_ref, gate_ref, up_ref, down_ref, out_ref,
    tok, wg, wu, wd, place, send, recv, rows, hidden, stacked, ysend, yrecv, part,
    tok_sem, w_sem, self_sem, send_sem, recv_sem, yself_sem, ysend_sem, yrecv_sem,
):
    devices = groups * loc_ranks
    tok_dev = tok.shape[0] // quarters
    quarter = tok.shape[1]
    slots = devices * cap
    z, l = lax.axis_index("grp"), lax.axis_index("loc")
    me = z * loc_ranks + l

    def token_copy(q):
        return pltpu.make_async_copy(
            tokens_ref.at[:, pl.ds(q * quarter, quarter)],
            tok.at[pl.ds(q * tok_dev, tok_dev)],
            tok_sem.at[q],
        )

    def weight_copy(m, j):
        from_ref, to_ref = ((gate_ref, wg), (up_ref, wu), (down_ref, wd))[m]
        return pltpu.make_async_copy(
            from_ref.at[:, pl.ds(j * FF, FF)], to_ref.at[j], w_sem.at[m, j]
        )

    for q in range(quarters):
        token_copy(q).start()
    def each_peer(act):
        mirror = groups - 1 - z
        for zz, first in (
            [(mirror, 0)]
            + [(lax.rem(mirror + d, groups), 0) for d in range(1, groups)]
        ):
            def step(d, carry, zz=zz):
                ll = lax.rem(l + d, loc_ranks)

                @pl.when(zz * loc_ranks + ll != me)
                def _():
                    act(zz, ll, zz * loc_ranks + ll)

                return carry

            lax.fori_loop(first, loc_ranks, step, 0)

    barrier = pltpu.get_barrier_semaphore()

    def greet(zz, ll, peer):
        pl.semaphore_signal(
            barrier, inc=1, device_id={"grp": zz, "loc": ll}, device_id_type=MESH
        )

    each_peer(greet)

    ids = ids_ref[...]
    inside = ids < EXP_WIN
    expert = jnp.min(jnp.where(inside, ids, EXP_WIN), 0, keepdims=True)
    onehot = (iota((EXP_WIN, tok_dev), 0) == expert).astype(jnp.float32)
    earlier = (iota((tok_dev, tok_dev), 0) < iota((tok_dev, tok_dev), 1)).astype(jnp.bfloat16)
    before = jnp.dot(onehot.astype(jnp.bfloat16), earlier, preferred_element_type=jnp.float32)
    rank = jnp.sum(before * onehot, 0, keepdims=True).astype(jnp.int32)
    weight_row = jnp.sum(jnp.where(inside, weight_ref[...], 0.0), 0, keepdims=True)
    diagonal = iota((tok_dev, tok_dev), 0) == iota((tok_dev, tok_dev), 1)
    weight = jnp.sum(jnp.where(diagonal, weight_row, 0.0), 1, keepdims=True)
    for j in range(own_exp):
        for q in range(quarters):
            target = jnp.where(
                (expert & (own_exp - 1)) == j,
                quotient(expert, own_exp) * TILE + q * cap + rank,
                -1,
            )
            place[j, :, pl.ds(q * tok_dev, tok_dev)] = (
                iota((devices * TILE, tok_dev), 0) == target
            ).astype(jnp.bfloat16)

    for q in range(quarters):
        token_copy(q).wait()

    def forward(j, zz, ll, peer):
        return pltpu.make_async_remote_copy(
            src_ref=send.at[j, peer], dst_ref=recv.at[j, me],
            send_sem=send_sem.at[j, peer], recv_sem=recv_sem.at[j, me],
            device_id={"grp": zz, "loc": ll}, device_id_type=MESH,
        )

    def arrived(j, zz, ll, peer):
        return pltpu.make_async_remote_copy(
            src_ref=send.at[j, peer], dst_ref=recv.at[j, peer],
            send_sem=send_sem.at[j, peer], recv_sem=recv_sem.at[j, peer],
            device_id={"grp": zz, "loc": ll}, device_id_type=MESH,
        )

    def back(j, zz, ll, peer):
        return pltpu.make_async_remote_copy(
            src_ref=ysend.at[j, peer], dst_ref=yrecv.at[j, me],
            send_sem=ysend_sem.at[j, peer], recv_sem=yrecv_sem.at[j, me],
            device_id={"grp": zz, "loc": ll}, device_id_type=MESH,
        )

    def returned(j, zz, ll, peer):
        return pltpu.make_async_remote_copy(
            src_ref=ysend.at[j, peer], dst_ref=yrecv.at[j, peer],
            send_sem=ysend_sem.at[j, peer], recv_sem=yrecv_sem.at[j, peer],
            device_id={"grp": zz, "loc": ll}, device_id_type=MESH,
        )

    def own_forward(j):
        return pltpu.make_async_copy(send.at[j, me], recv.at[j, me], self_sem.at[j])

    def own_back(j):
        return pltpu.make_async_copy(ysend.at[j, me], yrecv.at[j, me], yself_sem.at[j])

    for j in range(own_exp):
        picked = jnp.dot(place[j], tok[...], preferred_element_type=jnp.float32)
        send[j] = picked.astype(jnp.bfloat16).reshape(devices, TILE, quarter)
        if j == 0:
            pl.semaphore_wait(barrier, devices - 1)
        each_peer(lambda zz, ll, peer: forward(j, zz, ll, peer).start())
        own_forward(j).start()
        for m in range(3):
            weight_copy(m, j).start()

    col = iota((1, devices * TILE), 1)
    home = quotient(col & (slots - 1), cap) * TILE + quotient(col, slots) * cap + (col & (cap - 1))
    gather_in = (iota((devices * TILE, devices * TILE), 0) == home).astype(jnp.bfloat16)
    home = quotient(col & (TILE - 1), cap) * slots + quotient(col, TILE) * cap + (col & (cap - 1))
    spread_out = (iota((devices * TILE, devices * TILE), 0) == home).astype(jnp.bfloat16)

    step = 256
    for j in range(own_exp):
        each_peer(lambda zz, ll, peer: arrived(j, zz, ll, peer).wait_recv())
        own_forward(j).wait()
        ordered = jnp.dot(
            spread_out, recv[j].reshape(devices * TILE, quarter),
            preferred_element_type=jnp.float32,
        ).astype(jnp.bfloat16)
        for q in range(quarters):
            rows[:, pl.ds(q * quarter, quarter)] = ordered[q * slots : (q + 1) * slots]
        weight_copy(0, j).wait()
        weight_copy(1, j).wait()

        def gate_up(n, carry):
            at = pl.ds(pl.multiple_of(n * step, step), step)
            gate = jnp.dot(rows[...], wg[j, :, at], preferred_element_type=jnp.float32)
            up = jnp.dot(rows[...], wu[j, :, at], preferred_element_type=jnp.float32)
            hidden[:, at] = (gate / (1.0 + jnp.exp(-gate)) * up).astype(jnp.bfloat16)
            return carry

        lax.fori_loop(0, FF // step, gate_up, 0)
        weight_copy(2, j).wait()

        def down(q, carry):
            product = lax.dot_general(
                hidden[...], wd[j, pl.ds(pl.multiple_of(q * quarter, quarter), quarter), :],
                (((1,), (1,)), ((), ())), preferred_element_type=jnp.float32,
            )
            stacked[pl.ds(pl.multiple_of(q * slots, slots), slots), :] = product.astype(jnp.bfloat16)
            return carry

        lax.fori_loop(0, quarters, down, 0)
        ysend[j] = (
            jnp.dot(gather_in, stacked[...], preferred_element_type=jnp.float32)
            .astype(jnp.bfloat16)
            .reshape(devices, TILE, quarter)
        )
        each_peer(lambda zz, ll, peer: back(j, zz, ll, peer).start())
        own_back(j).start()

    for j in range(own_exp):
        each_peer(lambda zz, ll, peer: returned(j, zz, ll, peer).wait_recv())
        own_back(j).wait()
        blocks = yrecv[j].reshape(devices * TILE, quarter)
        for q in range(quarters):
            at = pl.ds(q * quarter, quarter)
            chosen = lax.dot_general(
                place[j, :, pl.ds(q * tok_dev, tok_dev)], blocks,
                (((0,), (0,)), ((), ())), preferred_element_type=jnp.float32,
            )
            if j > 0:
                chosen = chosen + part[:, at].astype(jnp.float32)
            if j < own_exp - 1:
                part[:, at] = chosen.astype(jnp.bfloat16)
            else:
                out_ref[:, at] = (chosen * weight).astype(jnp.bfloat16)

    for j in range(own_exp):
        each_peer(lambda zz, ll, peer: forward(j, zz, ll, peer).wait_send())
        each_peer(lambda zz, ll, peer: back(j, zz, ll, peer).wait_send())


def whole_experts(tokens, expert_ids, route_weights, w_gate, w_up, w_down):
    tok_dev, width = tokens.shape
    cap = tok_dev // EXP_WIN
    groups, loc_ranks = lax.axis_size("grp"), lax.axis_size("loc")
    devices = groups * loc_ranks
    own_exp = w_gate.shape[1] // FF
    quarters = TILE // cap
    quarter = width // quarters
    slots = devices * cap
    bf16 = jnp.bfloat16
    anywhere, vmem = pl.BlockSpec(memory_space=pl.ANY), pl.BlockSpec(memory_space=pltpu.VMEM)
    dma = pltpu.SemaphoreType.DMA
    block = pltpu.VMEM((own_exp, devices, TILE, quarter), bf16)
    return pl.pallas_call(
        functools.partial(experts_kernel, groups, loc_ranks, own_exp, cap, quarters),
        out_shape=jax.ShapeDtypeStruct((tok_dev, width), bf16),
        in_specs=[vmem, vmem, anywhere, anywhere, anywhere, anywhere],
        out_specs=vmem,
        scratch_shapes=[
            pltpu.VMEM((quarters * tok_dev, quarter), bf16),
            pltpu.VMEM((own_exp, width, FF), bf16),
            pltpu.VMEM((own_exp, width, FF), bf16),
            pltpu.VMEM((own_exp, width, FF), bf16),
            pltpu.VMEM((own_exp, devices * TILE, quarters * tok_dev), bf16),
            block,
            block,
            pltpu.VMEM((slots, width), bf16),
            pltpu.VMEM((slots, FF), bf16),
            pltpu.VMEM((quarters * slots, quarter), bf16),
            block,
            block,
            pltpu.VMEM((tok_dev, width), bf16),
            dma((quarters,)),
            dma((3, own_exp)),
            dma((own_exp,)),
            dma((own_exp, devices)),
            dma((own_exp, devices)),
            dma((own_exp,)),
            dma((own_exp, devices)),
            dma((own_exp, devices)),
        ],
        compiler_params=pltpu.CompilerParams(
            collective_id=0, has_side_effects=True, vmem_limit_bytes=60 * 2**20
        ),
        cost_estimate=pl.CostEstimate(
            flops=6 * slots * own_exp * width * FF,
            bytes_accessed=6 * own_exp * width * FF,
            transcendentals=slots * own_exp * FF,
        ),
    )(expert_ids.T, route_weights.T, tokens, w_gate, w_up, w_down)


def send_back(partial_value):
    return lax.all_to_all(partial_value, "grp", split_axis=0, concat_axis=0, tiled=True)


def split_experts(tokens, expert_ids, route_weights, w_gate, w_up, w_down):
    tok_dev, model_width = tokens.shape
    capacity = tok_dev // EXP_WIN
    groups = lax.axis_size("grp")
    loc_ranks = lax.axis_size("loc")
    hid_dev = w_gate.shape[1]
    hid_grp = hid_dev * loc_ranks
    hid_exp = min(FF, hid_grp)
    per_grp = hid_grp // hid_exp
    spread = FF // hid_exp
    slot_count = EXP_WIN * spread * capacity
    flat_ids = expert_ids.reshape(-1)
    flat_weight = route_weights.reshape(-1)
    owner_tok = jnp.arange(flat_ids.shape[0], dtype=jnp.int32) // expert_ids.shape[1]
    inside = flat_ids < EXP_WIN
    onehot = (
        (flat_ids[:, None] == jnp.arange(EXP_WIN, dtype=jnp.int32)[None, :]) & inside[:, None]
    ).astype(jnp.int32)
    before = jnp.cumsum(onehot, 0) - onehot
    rank_in = jnp.sum(before * onehot, 1)
    slot_tok = jnp.full((slot_count + 1,), tok_dev, jnp.int32)
    slot_weight = jnp.zeros((slot_count + 1,), jnp.float32)
    for copy_idx in range(spread):
        where_to = jnp.where(
            inside, (flat_ids * spread + copy_idx) * capacity + rank_in, slot_count
        )
        slot_tok = slot_tok.at[where_to].set(owner_tok)
        slot_weight = slot_weight.at[where_to].set(flat_weight)
    slot_tok = slot_tok[:slot_count]
    slot_weight = slot_weight[:slot_count]
    padded = jnp.concatenate([tokens, jnp.zeros((1, model_width), tokens.dtype)], 0)
    outgoing = padded[slot_tok].reshape(groups, per_grp, capacity, model_width)
    full_down = lax.all_gather(w_down, "loc", axis=1, tiled=True)
    down_cols = full_down.reshape(model_width, per_grp, hid_exp)
    own_exp = max(1, hid_dev // hid_exp)
    own_width = min(hid_dev, hid_exp)
    first_exp = lax.axis_index("loc") * hid_dev // hid_exp
    gate_cols = w_gate.reshape(model_width, own_exp, own_width)
    up_cols = w_up.reshape(model_width, own_exp, own_width)
    everyone = lax.all_gather(
        lax.all_to_all(outgoing, "grp", split_axis=0, concat_axis=0, tiled=True),
        "loc",
        axis=0,
        tiled=True,
    )
    own_rows = lax.dynamic_slice_in_dim(everyone, first_exp, own_exp, 1)
    gate_act = jnp.einsum("njkd,dji->nkji", own_rows, gate_cols, preferred_element_type=jnp.float32)
    up_act = jnp.einsum("njkd,dji->nkji", own_rows, up_cols, preferred_element_type=jnp.float32)
    hidden = (jax.nn.silu(gate_act) * up_act).astype(jnp.bfloat16)
    hidden = hidden.reshape(hidden.shape[0], hidden.shape[1], own_exp * own_width)
    shared = lax.all_to_all(hidden, "loc", split_axis=0, concat_axis=2, tiled=True)
    shared = shared.reshape(shared.shape[0], shared.shape[1], per_grp, hid_exp)
    partial_value = jnp.einsum(
        "skje,dje->sjkd", shared, down_cols, preferred_element_type=jnp.float32
    )
    returned = send_back(partial_value)
    returned = returned.reshape(slot_count, model_width)
    combined = (
        jnp.zeros((tok_dev + 1, model_width), jnp.float32)
        .at[slot_tok]
        .add(returned * slot_weight[:, None])
    )
    return combined[:tok_dev].astype(jnp.bfloat16)


def local(tokens, expert_ids, route_weights, w_gate, w_up, w_down):
    tok_dev, width = tokens.shape
    devices = lax.axis_size("grp") * lax.axis_size("loc")
    cap = tok_dev // EXP_WIN
    whole = (
        w_gate.shape[1] % FF == 0
        and devices * w_gate.shape[1] == EXP_WIN * FF
        and tok_dev % EXP_WIN == 0
        and tok_dev % 128 == 0
        and TILE % cap == 0
        and devices & (devices - 1) == 0
        and width % (128 * (TILE // cap)) == 0
    )
    plan = whole_experts if whole else split_experts
    return plan(tokens, expert_ids, route_weights, w_gate, w_up, w_down)


def solution(mesh):
    placed = (
        P(("rep", "grp", "loc"), None),
        P(("rep", "grp", "loc"), None),
        P(("rep", "grp", "loc"), None),
        P(None, ("grp", "loc")),
        P(None, ("grp", "loc")),
        P(None, ("grp", "loc")),
    )
    return jax.shard_map(
        local, mesh=mesh, in_specs=placed, out_specs=P(("rep", "grp", "loc"), None), check_vma=False
    )
```
